512 devices in a mesh: rep: 8 (over x, y_lo), fsdp: 64 (over z, y_hi, core).
Axes of the slice: x: 4, y: 8 (y_hi: 4, y_lo: 2; y = y_hi * 2 + y_lo), z: 8, core: 2. Of those that a mesh axis runs over, the one named last changes fastest.
Arguments:
- tokens_in: bfloat16 [8, 2048, 2048], P('rep', 'fsdp'), may hold values from -6 to 6
- out_grad: bfloat16 [8, 2048, 2048], P('rep', 'fsdp'), may hold values from -18 to 18
- gate_weight: bfloat16 [8, 4096, 2048], P('rep', 'fsdp'), may hold values from -6.1 to 6.1
- up_weight: bfloat16 [8, 4096, 2048], P('rep', 'fsdp'), may hold values from -6 to 6
- down_weight: bfloat16 [8, 4096, 2048], P('rep', 'fsdp'), may hold values from -20 to 20
- base_gate: bfloat16 [4096, 2048], P('fsdp'), may hold values from -6 to 6
- first_moment: float32 [8, 4096, 2048], P('rep', 'fsdp'), may hold values from -3 to 3
- second_moment: float32 [8, 4096, 2048], P('rep', 'fsdp'), may hold values from 0.05 to 1
- outer_momentum: float32 [4096, 2048], P('fsdp'), may hold values from -0.18 to 0.18
Outputs:
- new_base: float32 [4096, 2048], P('fsdp')
- new_momentum: float32 [4096, 2048], P('fsdp')
- first_out: float32 [8, 4096, 2048], P('rep', 'fsdp')
- second_out: float32 [8, 4096, 2048], P('rep', 'fsdp')
The draws below stay inside these ranges and needn't reach their ends.
All inputs are finite; a program needn't handle non-finite values.
Results may differ from the reference program's by a relative error of at most 0.0033.
Values may be sent and summed in bfloat16 or wider, within the bound.
A program may use at most 64 MiB of HBM per device.

```python
import math
import jax
import jax.numpy as jnp
from jax import lax

D = 2048
REP = 8
FF = 4096
TOK = 2048
N_REP = 8


def shared_base(key):
    normal_part = jnp.clip(jax.random.normal(key, (FF, D), jnp.float32), -6.0, 6.0)
    return normal_part


def draw_base_gate(key, part):
    return shared_base(key).astype(jnp.bfloat16)


def draw_gate_weight(key, part):
    centre = shared_base(key)
    key = jax.random.fold_in(key, 21)
    noise = jnp.clip(jax.random.normal(key, (REP, FF, D), jnp.float32), -4.0, 4.0) * 0.02
    return (centre[None] + noise).astype(jnp.bfloat16)


def draw_down_weight(key, part):
    key = jax.random.fold_in(key, 37)
    scale_key, entry_key = jax.random.split(key)
    scales = jnp.exp(jax.random.uniform(scale_key, (REP, FF, 1), jnp.float32, math.log(0.5), math.log(5.0)))
    entries = jnp.clip(jax.random.normal(entry_key, (REP, FF, D), jnp.float32), -4.0, 4.0)
    return (entries * scales).astype(jnp.bfloat16)


def level_of(rng, shape, shards, least, top_value):
    level = 1.0
    for dim, shards_of in shards:
        draws = jax.random.uniform(jax.random.fold_in(jax.random.fold_in(rng, 6), dim), (shards_of,), jnp.float32, least / len(shards), top_value / len(shards))
        level = level * jnp.repeat(jnp.exp(draws), shape[dim] // shards_of).reshape((-1,) + (1,) * (len(shape) - 1 - dim))
    return level


def bell_draw(key, dims, scale, reach, shards=(), kind=jnp.bfloat16):
    drawn = jax.random.normal(key, dims, jnp.float32) * scale
    if len(shards) > 0:
        drawn = level_of(key, dims, shards, -0.22, 0.18) * drawn
    return jnp.clip(drawn, min=-reach, max=reach).astype(kind)


def setup_inputs(seed: int = 0) -> dict:
    streams_of = jax.random.split(jax.random.key(seed), 10)
    return {
        "tokens_in": bell_draw(streams_of[0], (REP, TOK, D), 1.0, 6.0, ((0, 8), (1, 64))),
        "out_grad": bell_draw(streams_of[1], (REP, TOK, D), 3.0, 18.0, ((0, 8), (1, 64))),
        "gate_weight": draw_gate_weight(jax.random.fold_in(streams_of[9], 71), 0),
        "up_weight": bell_draw(streams_of[3], (REP, FF, D), 1.0, 6.0, ((0, 8), (1, 64))),
        "down_weight": draw_down_weight(jax.random.fold_in(streams_of[9], 71), 0),
        "base_gate": draw_base_gate(jax.random.fold_in(streams_of[9], 71), 0),
        "first_moment": bell_draw(streams_of[6], (REP, FF, D), 0.5, 3.0, ((0, 8), (1, 64)), jnp.float32),
        "second_moment": jnp.clip(jnp.exp(math.log(1.0) - 2.9957323 * jax.random.uniform(streams_of[7], (REP, FF, D), jnp.float32) ** level_of(streams_of[7], (REP, FF, D), ((0, 8), (1, 64)), -0.2, 0.2)), 0.05, 1.0),
        "outer_momentum": bell_draw(streams_of[8], (FF, D), 0.03, 0.18, ((0, 64),), jnp.float32),
    }


inner_rate = 0.02
beta_first = 0.9
beta_second = 0.95
adam_floor = 1e-08
decay_rate = 0.1
bias_first = 1.0 - 0.9 ** 20
bias_second = 1.0 - 0.95 ** 20
nesterov_factor = 0.9
outer_rate = 0.7

def replica_step(packed):
    rows, grads, gate, up, down, moment, second = packed
    in_scale = 1.0 / math.sqrt(D)
    out_scale = 1.0 / math.sqrt(FF)
    pre = jnp.dot(rows, gate.T, preferred_element_type=jnp.float32) * in_scale
    lin = jnp.dot(rows, up.T, preferred_element_type=jnp.float32) * in_scale
    back = jnp.dot(grads, down.T, preferred_element_type=jnp.float32) * out_scale
    sig = jax.nn.sigmoid(pre)
    dpre = (back * lin * sig * (1.0 + pre * (1.0 - sig))).astype(jnp.bfloat16)
    grad = jnp.dot(dpre.T, rows, preferred_element_type=jnp.float32) * in_scale
    moment_new = beta_first * moment + (1.0 - beta_first) * grad
    second_new = beta_second * second + (1.0 - beta_second) * grad * grad
    direction = moment_new / bias_first / (jnp.sqrt(second_new / bias_second) + adam_floor)
    inner = gate.astype(jnp.float32) * (1.0 - inner_rate * decay_rate) - inner_rate * direction
    return (inner, moment_new, second_new)

def reference(tokens_in, out_grad, gate_weight, up_weight, down_weight, base_gate, first_moment, second_moment, outer_momentum):
    inner, first_out, second_out = lax.map(replica_step, (tokens_in, out_grad, gate_weight, up_weight, down_weight, first_moment, second_moment))
    base_value = base_gate.astype(jnp.float32)

    def add_group(total, inner_one):
        return (total + (base_value - inner_one), None)
    total, unused = lax.scan(add_group, jnp.zeros(base_value.shape, jnp.float32), inner)
    outer_grad = total / N_REP
    new_momentum = nesterov_factor * outer_momentum + outer_grad
    new_base = base_value - outer_rate * (outer_grad + nesterov_factor * new_momentum)
    return (new_base, new_momentum, first_out, second_out)
```

```python
import math

import jax
import jax.numpy as jnp
from jax import lax
from jax.experimental import pallas as pl
from jax.experimental.pallas import tpu as pltpu
from jax.sharding import PartitionSpec as P

inner_rate = 0.02
beta_first = 0.9
beta_second = 0.95
adam_floor = 1e-08
decay_rate = 0.1
bias_first = 1.0 - 0.9**20
bias_second = 1.0 - 0.95**20
nesterov_factor = 0.9
outer_rate = 0.7

MESH = pl.DeviceIdType.MESH
NZ, NY, REP = 8, 4, 8
ROWS, UNITS, D = 32, 64, 2048
SLOT = 4 * ROWS
CHUNK = 16
N_CHUNK = UNITS // CHUNK
COLS = D // REP

in_scale = 1.0 / math.sqrt(D)
out_scale = 1.0 / math.sqrt(UNITS * NZ * NY * 2)


def place(way, hops):
    if hops == 0:
        return 0
    if hops == NZ // 2:
        return 1
    return 2 * hops + way


def kernel(
    tokens, grads, gate, up, down, base, first, second,
    grad_out, total_out,
    xg, wp, wd, acc, base_v, first_v, second_v, gsend, grecv, grad_v, diff, rs, ag,
    load_sem, zs, zr, cs, cr, ys, yr, ws, wr, gs, gr, ss, sr, as_, ar, out_sem,
):
    rep = lax.axis_index("rep")
    me = lax.axis_index("fsdp")
    z = me // (2 * NY)
    y = (me // 2) % NY
    core = me % 2

    def at(z_, y_, core_):
        return (rep, (z_ * NY + y_) * 2 + core_)

    z_next = (at((z + 1) % NZ, y, core), at((z + NZ - 1) % NZ, y, core))
    sibling = at(z, y, 1 - core)
    token_pair = at(z, y + 1 - 2 * (y % 2), core)
    weight_pair = at(z, (y + 3 + 2 * (y % 2)) % NY, core)
    peers = [((rep + k) % REP, me) for k in range(1, REP)]

    loads = [
        pltpu.make_async_copy(src, dst, load_sem.at[i])
        for i, (src, dst) in enumerate(
            [
                (tokens.at[0], xg.at[0, pl.ds(0, ROWS)]),
                (grads.at[0], xg.at[1, pl.ds(0, ROWS)]),
                (gate.at[0], wp.at[pl.ds(0, UNITS)]),
                (up.at[0], wp.at[pl.ds(2 * UNITS, UNITS)]),
                (down.at[0], wd.at[pl.ds(0, UNITS)]),
                (base, base_v),
                (first.at[0], first_v),
                (second.at[0], second_v),
            ]
        )
    ]
    for load in loads:
        load.start()

    barrier = pltpu.get_barrier_semaphore()
    others = [*z_next, sibling, token_pair, weight_pair, *peers]
    for other in others:
        pl.semaphore_signal(barrier, inc=1, device_id=other, device_id_type=MESH)
    for load in loads[:5]:
        load.wait()
    pl.semaphore_wait(barrier, len(others))

    def remote(src, dst, send, recv, device):
        return pltpu.make_async_remote_copy(
            src_ref=src, dst_ref=dst, send_sem=send, recv_sem=recv, device_id=device, device_id_type=MESH
        )

    def shard(kind, slot, yy, cc):
        return xg.at[kind, pl.ds(slot * SLOT + yy * 2 * ROWS + cc * ROWS, ROWS)]

    def z_copy(way, yy, hops, kind):
        return remote(
            shard(kind, place(way, hops - 1), yy, 0),
            shard(kind, place(way, hops), yy, 0),
            zs.at[way, yy, hops - 1, kind],
            zr.at[way, yy, hops - 1, kind],
            z_next[way],
        )

    def core_copy(slot, yy, kind):
        return remote(
            shard(kind, slot, yy, 0), shard(kind, slot, yy, 1), cs.at[slot, yy, kind], cr.at[slot, yy, kind], sibling
        )

    def y_copy(kind):
        return remote(shard(kind, 0, 0, 0), shard(kind, 0, 1, 0), ys.at[kind], yr.at[kind], token_pair)

    def w_copy(i):
        ref, row = ((wp, 0), (wp, 2 * UNITS), (wd, 0))[i]
        return remote(
            ref.at[pl.ds(row, UNITS)], ref.at[pl.ds(row + UNITS, UNITS)], ws.at[i], wr.at[i], weight_pair
        )

    sent = []

    def start(copy):
        copy.start()
        sent.append(copy)

    for kind in range(2):
        start(y_copy(kind))
        for way in range(2):
            start(z_copy(way, 0, 1, kind))
    for i in range(3):
        start(w_copy(i))
    for kind in range(2):
        start(core_copy(0, 0, kind))

    def arrive(yy, hops):
        for kind in range(2):
            for way in range(2):
                if hops == NZ // 2 and kind != way:
                    continue
                z_copy(way, yy, hops, kind).wait_recv()
                if hops + 1 < NZ // 2 or (hops + 1 == NZ // 2 and kind == way):
                    start(z_copy(way, yy, hops + 1, kind))
                start(core_copy(place(way, hops), yy, kind))

    arrive(0, 1)
    arrive(0, 2)
    for kind in range(2):
        y_copy(kind).wait_recv()
        for way in range(2):
            start(z_copy(way, 1, 1, kind))
        start(core_copy(0, 1, kind))
    arrive(1, 1)
    arrive(0, 3)
    arrive(1, 2)
    arrive(0, 4)
    arrive(1, 3)

    nt = (((1,), (1,)), ((), ()))

    def block(slot, slots, begin):
        for s in range(slot, slot + slots):
            for yy in range(2):
                for kind in range(2):
                    core_copy(s, yy, kind).wait_recv()
        rows = pl.ds(slot * SLOT, slots * SLOT)
        x = xg[0, rows]
        both = lax.dot_general(wp[...], x, nt, preferred_element_type=jnp.float32) * in_scale
        pre, lin = both[: 2 * UNITS], both[2 * UNITS :]
        back = lax.dot_general(wd[...], xg[1, rows], nt, preferred_element_type=jnp.float32) * out_scale
        sig = jax.nn.sigmoid(pre)
        dpre = (back * lin * sig * (1.0 + pre * (1.0 - sig))).astype(jnp.bfloat16)
        part = jnp.dot(dpre, x, preferred_element_type=jnp.float32)
        if begin:
            acc[...] = part
        else:
            acc[...] += part

    for i in range(3):
        w_copy(i).wait_recv()
    block(0, 1, True)
    block(2, 2, False)
    block(4, 2, False)
    block(6, 2, False)
    arrive(1, 4)
    block(1, 1, False)

    def g_copy(c):
        rows = pl.ds(c * CHUNK, CHUNK)
        return remote(gsend.at[rows], grecv.at[rows], gs.at[c], gr.at[c], weight_pair)

    for c in range(N_CHUNK):
        gsend[pl.ds(c * CHUNK, CHUNK)] = acc[pl.ds(UNITS + c * CHUNK, CHUNK)].astype(jnp.bfloat16)
        start(g_copy(c))
    for load in loads[5:]:
        load.wait()

    mine = pl.ds(pl.multiple_of(rep * COLS, COLS), COLS)

    def rs_copy(c, k):
        rows = pl.ds(c * CHUNK, CHUNK)
        cols = pl.ds(pl.multiple_of(((rep + k) % REP) * COLS, COLS), COLS)
        return remote(diff.at[rows, cols], rs.at[k - 1, rows], ss.at[c, k - 1], sr.at[c, k - 1], peers[k - 1])

    def ag_copy(c, k):
        rows = pl.ds(c * CHUNK, CHUNK)
        return remote(ag.at[rows, mine], ag.at[rows, mine], as_.at[c, k - 1], ar.at[c, k - 1], peers[k - 1])

    outs = []

    def sum_chunk(c):
        rows = pl.ds(c * CHUNK, CHUNK)
        total = diff[rows, mine]
        for k in range(1, REP):
            rs_copy(c, k).wait_recv()
            total += rs[k - 1, rows]
        ag[rows, mine] = total / REP
        for k in range(1, REP):
            start(ag_copy(c, k))

    for c in range(N_CHUNK):
        rows = pl.ds(c * CHUNK, CHUNK)
        g_copy(c).wait_recv()
        grad = (acc[rows] + grecv[rows].astype(jnp.float32)) * in_scale
        grad_v[rows] = grad
        moment_new = beta_first * first_v[rows] + (1.0 - beta_first) * grad
        second_new = beta_second * second_v[rows] + (1.0 - beta_second) * grad * grad
        direction = moment_new / bias_first / (jnp.sqrt(second_new / bias_second) + adam_floor)
        gate_value = wp[rows].astype(jnp.float32)
        inner = gate_value * (1.0 - inner_rate * decay_rate) - inner_rate * direction
        diff[rows] = base_v[rows].astype(jnp.float32) - inner
        for k in range(1, REP):
            start(rs_copy(c, k))
        out = pltpu.make_async_copy(grad_v.at[rows], grad_out.at[rows], out_sem.at[0, c])
        out.start()
        outs.append(out)
        if c > 0:
            sum_chunk(c - 1)
    sum_chunk(N_CHUNK - 1)

    for c in range(N_CHUNK):
        rows = pl.ds(c * CHUNK, CHUNK)
        for k in range(1, REP):
            ag_copy(c, k).wait_recv()
        out = pltpu.make_async_copy(ag.at[rows], total_out.at[rows], out_sem.at[1, c])
        out.start()
        outs.append(out)
    for copy in sent:
        copy.wait_send()
    for out in outs:
        out.wait()


def on_device(
    tokens_in,
    out_grad,
    gate_weight,
    up_weight,
    down_weight,
    base_gate,
    first_moment,
    second_moment,
    outer_momentum,
):
    dma = pltpu.SemaphoreType.DMA
    f32, bf16 = jnp.float32, jnp.bfloat16
    grad, outer_grad = pl.pallas_call(
        kernel,
        out_shape=[jax.ShapeDtypeStruct((UNITS, D), f32)] * 2,
        in_specs=[pl.BlockSpec(memory_space=pl.ANY)] * 8,
        out_specs=[pl.BlockSpec(memory_space=pl.ANY)] * 2,
        scratch_shapes=[
            pltpu.VMEM((2, NZ * SLOT, D), bf16),
            pltpu.VMEM((4 * UNITS, D), bf16),
            pltpu.VMEM((2 * UNITS, D), bf16),
            pltpu.VMEM((2 * UNITS, D), f32),
            pltpu.VMEM((UNITS, D), bf16),
            pltpu.VMEM((UNITS, D), f32),
            pltpu.VMEM((UNITS, D), f32),
            pltpu.VMEM((UNITS, D), bf16),
            pltpu.VMEM((UNITS, D), bf16),
            pltpu.VMEM((UNITS, D), f32),
            pltpu.VMEM((UNITS, D), f32),
            pltpu.VMEM((REP - 1, UNITS, COLS), f32),
            pltpu.VMEM((UNITS, D), f32),
            dma((8,)),
            dma((2, 2, NZ // 2, 2)),
            dma((2, 2, NZ // 2, 2)),
            dma((NZ, 2, 2)),
            dma((NZ, 2, 2)),
            dma((2,)),
            dma((2,)),
            dma((3,)),
            dma((3,)),
            dma((N_CHUNK,)),
            dma((N_CHUNK,)),
            dma((N_CHUNK, REP - 1)),
            dma((N_CHUNK, REP - 1)),
            dma((N_CHUNK, REP - 1)),
            dma((N_CHUNK, REP - 1)),
            dma((2, N_CHUNK)),
        ],
        compiler_params=pltpu.CompilerParams(
            collective_id=0, has_side_effects=True, vmem_limit_bytes=48 * 2**20
        ),
        name="window",
    )(
        tokens_in,
        out_grad,
        gate_weight,
        up_weight,
        down_weight,
        base_gate,
        first_moment,
        second_moment,
    )
    moment_new = beta_first * first_moment[0] + (1.0 - beta_first) * grad
    second_new = beta_second * second_moment[0] + (1.0 - beta_second) * grad * grad
    new_momentum = nesterov_factor * outer_momentum + outer_grad
    base_value = base_gate.astype(jnp.float32)
    new_base = base_value - outer_rate * (outer_grad + nesterov_factor * new_momentum)
    return (new_base, new_momentum, moment_new[None], second_new[None])


def solution(mesh):
    in_specs = (
        P("rep", "fsdp", None),
        P("rep", "fsdp", None),
        P("rep", "fsdp", None),
        P("rep", "fsdp", None),
        P("rep", "fsdp", None),
        P("fsdp", None),
        P("rep", "fsdp", None),
        P("rep", "fsdp", None),
        P("fsdp", None),
    )
    out_specs = (P("fsdp", None), P("fsdp", None), P("rep", "fsdp", None), P("rep", "fsdp", None))
    return jax.shard_map(
        on_device, mesh=mesh, in_specs=in_specs, out_specs=out_specs, check_vma=False
    )
```

```python
import math

import jax
import jax.numpy as jnp
from jax import lax
from jax.experimental import pallas as pl
from jax.experimental.pallas import tpu as pltpu
from jax.sharding import PartitionSpec as P

inner_rate = 0.02
beta_first = 0.9
beta_second = 0.95
adam_floor = 1e-08
decay_rate = 0.1
bias_first = 1.0 - 0.9**20
bias_second = 1.0 - 0.95**20
nesterov_factor = 0.9
outer_rate = 0.7

MESH = pl.DeviceIdType.MESH
NZ, NY, REP = 8, 4, 8
ROWS, UNITS, D = 32, 64, 2048
SLOT = 4 * ROWS
CHUNK = 16
N_CHUNK = UNITS // CHUNK
COLS = D // REP

in_scale = 1.0 / math.sqrt(D)
out_scale = 1.0 / math.sqrt(UNITS * NZ * NY * 2)


def place(way, hops):
    if hops == 0:
        return 0
    if hops == NZ // 2:
        return 1
    return 2 * hops + way


def kernel(
    tokens, grads, gate, up, down, base, first, second,
    grad_out, total_out,
    xg, wp, wd, acc, base_v, first_v, second_v, gsend, grecv, grad_v, diff, diff_b, rs, ag,
    load_sem, zs, zr, cs, cr, ys, yr, ws, wr, gs, gr, ss, sr, as_, ar, out_sem,
):
    rep = lax.axis_index("rep")
    me = lax.axis_index("fsdp")
    z = me // (2 * NY)
    y = (me // 2) % NY
    core = me % 2

    def at(z_, y_, core_):
        return (rep, (z_ * NY + y_) * 2 + core_)

    z_next = (at((z + 1) % NZ, y, core), at((z + NZ - 1) % NZ, y, core))
    sibling = at(z, y, 1 - core)
    token_pair = at(z, y + 1 - 2 * (y % 2), core)
    weight_pair = at(z, (y + 3 + 2 * (y % 2)) % NY, core)
    peers = [((rep + k) % REP, me) for k in range(1, REP)]

    loads = [
        pltpu.make_async_copy(src, dst, load_sem.at[i])
        for src, dst, i in [
            (tokens.at[0], xg.at[0, pl.ds(0, ROWS)], 0),
            (grads.at[0], xg.at[1, pl.ds(0, ROWS)], 0),
            (gate.at[0], wp.at[pl.ds(0, UNITS)], 0),
            (up.at[0], wp.at[pl.ds(2 * UNITS, UNITS)], 0),
            (down.at[0], wd.at[pl.ds(0, UNITS)], 0),
            (base, base_v, 1),
            (first.at[0], first_v, 2),
            (second.at[0], second_v, 3),
        ]
    ]
    for load in loads:
        load.start()

    barrier = pltpu.get_barrier_semaphore()
    others = [*z_next, sibling, token_pair, weight_pair, *peers]
    for other in others:
        pl.semaphore_signal(barrier, inc=1, device_id=other, device_id_type=MESH)
    pltpu.make_async_copy(wp, wp, load_sem.at[0]).wait()
    pl.semaphore_wait(barrier, len(others))

    def remote(src, dst, send, recv, device):
        return pltpu.make_async_remote_copy(
            src_ref=src, dst_ref=dst, send_sem=send, recv_sem=recv, device_id=device, device_id_type=MESH
        )

    def wait_bytes(ref, sem):
        pltpu.make_async_copy(ref, ref, sem).wait()

    def shard(kind, slot, yy, cc):
        return xg.at[kind, pl.ds(slot * SLOT + yy * 2 * ROWS + cc * ROWS, ROWS)]

    def z_copy(way, yy, hops, kind):
        return remote(
            shard(kind, place(way, hops - 1), yy, 0),
            shard(kind, place(way, hops), yy, 0),
            zs,
            zr.at[way, yy, hops - 1, kind],
            z_next[way],
        )

    def core_copy(slot, yy, kind):
        return remote(shard(kind, slot, yy, 0), shard(kind, slot, yy, 1), cs, cr.at[slot], sibling)

    def y_copy(kind):
        return remote(shard(kind, 0, 0, 0), shard(kind, 0, 1, 0), ys, yr.at[kind], token_pair)

    def w_copy(i):
        ref, row = ((wp, 0), (wp, 2 * UNITS), (wd, 0))[i]
        return remote(ref.at[pl.ds(row, UNITS)], ref.at[pl.ds(row + UNITS, UNITS)], ws, wr, weight_pair)

    for kind in range(2):
        y_copy(kind).start()
        for way in range(2):
            z_copy(way, 0, 1, kind).start()
    for i in range(3):
        w_copy(i).start()
    for kind in range(2):
        core_copy(0, 0, kind).start()

    def arrive(yy, hops):
        for kind in range(2):
            for way in range(2):
                if hops == NZ // 2 and kind != way:
                    continue
                z_copy(way, yy, hops, kind).wait_recv()
                if hops + 1 < NZ // 2 or (hops + 1 == NZ // 2 and kind == way):
                    z_copy(way, yy, hops + 1, kind).start()
                core_copy(place(way, hops), yy, kind).start()

    nt = (((1,), (1,)), ((), ()))

    def slopes(slot, slots):
        for s in range(slot, slot + slots):
            wait_bytes(xg.at[0, pl.ds(0, SLOT)], cr.at[s])
        rows = pl.ds(slot * SLOT, slots * SLOT)
        x = xg[0, rows]
        both = lax.dot_general(wp[...], x, nt, preferred_element_type=jnp.float32) * in_scale
        pre, lin = both[: 2 * UNITS], both[2 * UNITS :]
        back = lax.dot_general(wd[...], xg[1, rows], nt, preferred_element_type=jnp.float32) * out_scale
        sig = jax.nn.sigmoid(pre)
        return (back * lin * sig * (1.0 + pre * (1.0 - sig))).astype(jnp.bfloat16), x

    def block(slot, slots, begin=False):
        dpre, x = slopes(slot, slots)
        part = jnp.dot(dpre, x, preferred_element_type=jnp.float32)
        if begin:
            acc[...] = part
        else:
            acc[...] += part

    arrive(0, 1)
    arrive(0, 2)
    for kind in range(2):
        y_copy(kind).wait_recv()
        for way in range(2):
            z_copy(way, 1, 1, kind).start()
        core_copy(0, 1, kind).start()
    arrive(1, 1)
    arrive(0, 3)
    arrive(1, 2)
    arrive(0, 4)
    wait_bytes(wp.at[pl.ds(0, 3 * UNITS)], wr)
    block(0, 1, True)
    block(2, 2)
    block(4, 2)
    arrive(1, 3)
    block(6, 2)
    arrive(1, 4)

    def g_copy(c):
        rows = pl.ds(c * CHUNK, CHUNK)
        return remote(gsend.at[rows], grecv.at[rows], gs, gr.at[c], weight_pair)

    dpre, x = slopes(1, 1)
    part = jnp.dot(dpre[UNITS:], x, preferred_element_type=jnp.float32)
    gsend[...] = (acc[pl.ds(UNITS, UNITS)] + part).astype(jnp.bfloat16)
    for c in range(N_CHUNK):
        g_copy(c).start()
    acc[pl.ds(0, UNITS)] += jnp.dot(dpre[:UNITS], x, preferred_element_type=jnp.float32)
    for load in loads[5:]:
        load.wait()

    mine = pl.ds(pl.multiple_of(rep * COLS, COLS), COLS)

    def rs_copy(c, k):
        rows = pl.ds(c * CHUNK, CHUNK)
        cols = pl.ds(pl.multiple_of(((rep + k) % REP) * COLS, COLS), COLS)
        return remote(diff_b.at[rows, cols], rs.at[k - 1, rows], ss, sr.at[c], peers[k - 1])

    def ag_copy(c, k):
        rows = pl.ds(c * CHUNK, CHUNK)
        return remote(ag.at[rows, mine], ag.at[rows, mine], as_, ar.at[c], peers[k - 1])

    def sum_chunk(c):
        rows = pl.ds(c * CHUNK, CHUNK)
        wait_bytes(rs.at[:, rows], sr.at[c])
        total = diff[rows, mine]
        for k in range(1, REP):
            total += rs[k - 1, rows].astype(jnp.float32)
        ag[rows, mine] = (total / REP).astype(jnp.bfloat16)
        for k in range(1, REP):
            ag_copy(c, k).start()

    for c in range(N_CHUNK):
        rows = pl.ds(c * CHUNK, CHUNK)
        g_copy(c).wait_recv()
        grad = (acc[rows] + grecv[rows].astype(jnp.float32)) * in_scale
        grad_v[rows] = grad
        moment_new = beta_first * first_v[rows] + (1.0 - beta_first) * grad
        second_new = beta_second * second_v[rows] + (1.0 - beta_second) * grad * grad
        direction = moment_new / bias_first / (jnp.sqrt(second_new / bias_second) + adam_floor)
        gate_value = wp[rows].astype(jnp.float32)
        inner = gate_value * (1.0 - inner_rate * decay_rate) - inner_rate * direction
        difference = base_v[rows].astype(jnp.float32) - inner
        diff[rows] = difference
        diff_b[rows] = difference.astype(jnp.bfloat16)
        for k in range(1, REP):
            rs_copy(c, k).start()
        pltpu.make_async_copy(grad_v.at[rows], grad_out.at[rows], out_sem.at[0]).start()
        if c > 0:
            sum_chunk(c - 1)
    sum_chunk(N_CHUNK - 1)

    for c in range(N_CHUNK):
        rows = pl.ds(c * CHUNK, CHUNK)
        wait_bytes(ag.at[rows, pl.ds(0, D - COLS)], ar.at[c])
        pltpu.make_async_copy(ag.at[rows], total_out.at[rows], out_sem.at[1]).start()

    wait_bytes(xg.at[0, pl.ds(0, 28 * ROWS)], zs)
    wait_bytes(xg.at[0], cs)
    wait_bytes(xg.at[0, pl.ds(0, 2 * ROWS)], ys)
    wait_bytes(wp.at[pl.ds(0, 3 * UNITS)], ws)
    wait_bytes(gsend, gs)
    wait_bytes(diff_b.at[:, pl.ds(0, D - COLS)], ss)
    wait_bytes(diff_b.at[:, pl.ds(0, D - COLS)], as_)
    wait_bytes(grad_v, out_sem.at[0])
    wait_bytes(ag, out_sem.at[1])


def on_device(
    tokens_in,
    out_grad,
    gate_weight,
    up_weight,
    down_weight,
    base_gate,
    first_moment,
    second_moment,
    outer_momentum,
):
    dma = pltpu.SemaphoreType.DMA
    f32, bf16 = jnp.float32, jnp.bfloat16
    grad, total = pl.pallas_call(
        kernel,
        out_shape=[jax.ShapeDtypeStruct((UNITS, D), f32), jax.ShapeDtypeStruct((UNITS, D), bf16)],
        in_specs=[pl.BlockSpec(memory_space=pl.ANY)] * 8,
        out_specs=[pl.BlockSpec(memory_space=pl.ANY)] * 2,
        scratch_shapes=[
            pltpu.VMEM((2, NZ * SLOT, D), bf16),
            pltpu.VMEM((4 * UNITS, D), bf16),
            pltpu.VMEM((2 * UNITS, D), bf16),
            pltpu.VMEM((2 * UNITS, D), f32),
            pltpu.VMEM((UNITS, D), bf16),
            pltpu.VMEM((UNITS, D), f32),
            pltpu.VMEM((UNITS, D), f32),
            pltpu.VMEM((UNITS, D), bf16),
            pltpu.VMEM((UNITS, D), bf16),
            pltpu.VMEM((UNITS, D), f32),
            pltpu.VMEM((UNITS, D), f32),
            pltpu.VMEM((UNITS, D), bf16),
            pltpu.VMEM((REP - 1, UNITS, COLS), bf16),
            pltpu.VMEM((UNITS, D), bf16),
            dma((4,)),
            dma,
            dma((2, 2, NZ // 2, 2)),
            dma,
            dma((NZ,)),
            dma,
            dma((2,)),
            dma,
            dma,
            dma,
            dma((N_CHUNK,)),
            dma,
            dma((N_CHUNK,)),
            dma,
            dma((N_CHUNK,)),
            dma((2,)),
        ],
        compiler_params=pltpu.CompilerParams(
            collective_id=0, has_side_effects=True, vmem_limit_bytes=60 * 2**20
        ),
        name="window",
    )(
        tokens_in,
        out_grad,
        gate_weight,
        up_weight,
        down_weight,
        base_gate,
        first_moment,
        second_moment,
    )
    outer_grad = total.astype(f32)
    moment_new = beta_first * first_moment[0] + (1.0 - beta_first) * grad
    second_new = beta_second * second_moment[0] + (1.0 - beta_second) * grad * grad
    new_momentum = nesterov_factor * outer_momentum + outer_grad
    base_value = base_gate.astype(jnp.float32)
    new_base = base_value - outer_rate * (outer_grad + nesterov_factor * new_momentum)
    return (new_base, new_momentum, moment_new[None], second_new[None])


def solution(mesh):
    in_specs = (
        P("rep", "fsdp", None),
        P("rep", "fsdp", None),
        P("rep", "fsdp", None),
        P("rep", "fsdp", None),
        P("rep", "fsdp", None),
        P("fsdp", None),
        P("rep", "fsdp", None),
        P("rep", "fsdp", None),
        P("fsdp", None),
    )
    out_specs = (P("fsdp", None), P("fsdp", None), P("rep", "fsdp", None), P("rep", "fsdp", None))
    return jax.shard_map(
        on_device, mesh=mesh, in_specs=in_specs, out_specs=out_specs, check_vma=False
    )
```

```python
import math

import jax
import jax.numpy as jnp
from jax import lax
from jax.experimental import pallas as pl
from jax.experimental.pallas import tpu as pltpu
from jax.sharding import PartitionSpec as P

inner_rate = 0.02
beta_first = 0.9
beta_second = 0.95
adam_floor = 1e-08
decay_rate = 0.1
bias_first = 1.0 - 0.9**20
bias_second = 1.0 - 0.95**20
nesterov_factor = 0.9
outer_rate = 0.7

MESH = pl.DeviceIdType.MESH
NZ, NY, REP = 8, 4, 8
ROWS, UNITS, D = 32, 64, 2048
SLOT = 4 * ROWS
PIECE = 16
PIECES = 4
Y_FIRST = 3
CHUNK = 32
N_CHUNK = UNITS // CHUNK
COLS = D // REP

in_scale = 1.0 / math.sqrt(D)
out_scale = 1.0 / math.sqrt(UNITS * NZ * NY * 2)


def place(way, hops):
    if hops == 0:
        return 0
    if hops == NZ // 2:
        return 1
    return 2 * hops + way


def kernel(
    tokens, grads, gate, up, down, base, first, second,
    grad_out, total_out,
    xg, wp, wd, held_v, acc, base_v, first_v, second_v, gsend, grecv, grad_v, diff, diff_b, rs, ag,
    load_sem, zs, zr, cs, cr, ys, yr, ls, lr, ws, wr, gs, gr, ss, sr, as_, ar, out_sem,
):
    rep = lax.axis_index("rep")
    me = lax.axis_index("fsdp")
    z = me // (2 * NY)
    y = (me // 2) % NY
    core = me % 2

    def at(z_, y_, core_):
        return (rep, (z_ * NY + y_) * 2 + core_)

    z_next = (at((z + 1) % NZ, y, core), at((z + NZ - 1) % NZ, y, core))
    sibling = at(z, y, 1 - core)
    token_pair = at(z, y + 1 - 2 * (y % 2), core)
    weight_pair = at(z, (y + 3 + 2 * (y % 2)) % NY, core)
    peers = [((rep + k) % REP, me) for k in range(1, REP)]

    loads = [
        pltpu.make_async_copy(src, dst, load_sem.at[i])
        for src, dst, i in [
            (tokens.at[0], xg.at[0, pl.ds(0, ROWS)], 0),
            (grads.at[0], xg.at[1, pl.ds(0, ROWS)], 0),
            (gate.at[0], wp.at[pl.ds(0, UNITS)], 0),
            (up.at[0], wp.at[pl.ds(2 * UNITS, UNITS)], 0),
            (down.at[0], wd.at[pl.ds(0, UNITS)], 0),
            (base, base_v, 1),
            (first.at[0], first_v, 2),
            (second.at[0], second_v, 3),
        ]
    ]
    for load in loads:
        load.start()

    barrier = pltpu.get_barrier_semaphore()
    others = [*z_next, sibling, token_pair, weight_pair, *peers]
    for other in others:
        pl.semaphore_signal(barrier, inc=1, device_id=other, device_id_type=MESH)
    pltpu.make_async_copy(wp, wp, load_sem.at[0]).wait()
    pl.semaphore_wait(barrier, len(others))

    def remote(src, dst, send, recv, device):
        return pltpu.make_async_remote_copy(
            src_ref=src, dst_ref=dst, send_sem=send, recv_sem=recv, device_id=device, device_id_type=MESH
        )

    def wait_bytes(ref, sem):
        pltpu.make_async_copy(ref, ref, sem).wait()

    def shard(slot, yy, cc, p):
        row = slot * SLOT + yy * 2 * ROWS + cc * ROWS + p % 2 * PIECE
        return xg.at[p // 2, pl.ds(row, PIECE)]

    def goes(way, yy, hops, p):
        if yy == 1 and p >= Y_FIRST:
            return False
        return hops < NZ // 2 or (hops == NZ // 2 and (p >= (PIECES - yy) // 2) == way)

    def z_copy(way, yy, hops, p):
        return remote(
            shard(place(way, hops - 1), yy, 0, p),
            shard(place(way, hops), yy, 0, p),
            zs,
            zr.at[way, yy, hops - 1, p],
            z_next[way],
        )

    def core_copy(slot, yy, p):
        return remote(shard(slot, yy, 0, p), shard(slot, yy, 1, p), cs, cr.at[slot], sibling)

    def y_copy(p):
        return remote(shard(0, 0, 0, p), shard(0, 1, 0, p), ys, yr.at[p], token_pair)

    def late_copy(slot):
        return remote(shard(slot, 0, 0, Y_FIRST), shard(slot, 1, 0, Y_FIRST), ls, lr.at[slot], token_pair)

    def w_copy(i):
        ref, row = ((wp, 0), (wp, 2 * UNITS), (wd, 0))[i]
        return remote(ref.at[pl.ds(row, UNITS)], ref.at[pl.ds(row + UNITS, UNITS)], ws, wr.at[i // 2], weight_pair)

    order = (*range(Y_FIRST, PIECES), *range(Y_FIRST))
    for p in order:
        if p < Y_FIRST:
            y_copy(p).start()
        for way in range(2):
            z_copy(way, 0, 1, p).start()
    late_copy(0).start()
    for i in range(3):
        w_copy(i).start()
    for p in range(PIECES):
        core_copy(0, 0, p).start()

    def arrive(yy, hops):
        for p in order:
            for way in range(2):
                if not goes(way, yy, hops, p):
                    continue
                slot = place(way, hops)
                z_copy(way, yy, hops, p).wait_recv()
                if goes(way, yy, hops + 1, p):
                    z_copy(way, yy, hops + 1, p).start()
                if p >= Y_FIRST:
                    late_copy(slot).start()
                core_copy(slot, yy, p).start()

    def arrive_y():
        for p in range(Y_FIRST):
            y_copy(p).wait_recv()
            for way in range(2):
                z_copy(way, 1, 1, p).start()
            core_copy(0, 1, p).start()

    def arrive_late(hops):
        for way in range(2):
            if goes(way, 0, hops, Y_FIRST) and (hops > 0 or way == 0):
                slot = place(way, hops)
                late_copy(slot).wait_recv()
                core_copy(slot, 1, Y_FIRST).start()

    nt = (((1,), (1,)), ((), ()))

    def settle(slot, slots):
        for s in range(slot, slot + slots):
            wait_bytes(xg.at[0, pl.ds(0, SLOT)], cr.at[s])

    def gain(slot, slots, unit, units):
        x = xg[0, pl.ds(slot * SLOT, slots * SLOT)]
        if units == 2 * UNITS:
            both = lax.dot_general(wp[...], x, nt, preferred_element_type=jnp.float32) * in_scale
            pre, lin = both[:units], both[units:]
        else:
            pre = lax.dot_general(wp[pl.ds(unit, units)], x, nt, preferred_element_type=jnp.float32) * in_scale
            lin = lax.dot_general(wp[pl.ds(2 * UNITS + unit, units)], x, nt, preferred_element_type=jnp.float32) * in_scale
        sig = jax.nn.sigmoid(pre)
        return lin, sig, 1.0 + pre * (1.0 - sig)

    def slope(slot, slots, unit, units, held):
        rows = pl.ds(slot * SLOT, slots * SLOT)
        back = lax.dot_general(wd[pl.ds(unit, units)], xg[1, rows], nt, preferred_element_type=jnp.float32) * out_scale
        lin, sig, rest = held
        dpre = (back * lin * sig * rest).astype(jnp.bfloat16)
        return jnp.dot(dpre, xg[0, rows], preferred_element_type=jnp.float32)

    def partial(slot, slots, unit, units):
        return slope(slot, slots, unit, units, gain(slot, slots, unit, units))

    def early(slot, slots):
        settle(slot, slots)
        lin, sig, rest = gain(slot, slots, 0, 2 * UNITS)
        cols = pl.ds(slot * SLOT, slots * SLOT)
        held_v[:, cols] = lin * sig * rest

    def late(slot, slots, begin=False):
        rows = pl.ds(slot * SLOT, slots * SLOT)
        back = lax.dot_general(wd[...], xg[1, rows], nt, preferred_element_type=jnp.float32) * out_scale
        dpre = (back * held_v[:, rows]).astype(jnp.bfloat16)
        part = jnp.dot(dpre, xg[0, rows], preferred_element_type=jnp.float32)
        if begin:
            acc[...] = part
        else:
            acc[...] += part

    def block(slot, slots, begin=False):
        settle(slot, slots)
        part = partial(slot, slots, 0, 2 * UNITS)
        if begin:
            acc[...] = part
        else:
            acc[...] += part

    arrive(0, 1)
    arrive(0, 2)
    arrive_y()
    arrive_late(0)
    arrive(0, 3)
    arrive_late(1)
    arrive(1, 1)
    arrive(0, 4)
    arrive_late(2)
    wait_bytes(wd, wr.at[0])
    early(0, 1)
    arrive(1, 2)
    early(2, 2)
    early(4, 2)
    w_copy(2).wait_recv()
    late(0, 1, True)
    arrive_late(3)
    arrive(1, 3)
    late(2, 2)
    late(4, 2)
    block(6, 2)
    arrive_late(4)
    arrive(1, 4)

    def g_copy(c):
        rows = pl.ds(c * CHUNK, CHUNK)
        return remote(gsend.at[rows], grecv.at[rows], gs, gr.at[c], weight_pair)

    settle(1, 1)
    part = partial(1, 1, UNITS, UNITS)
    gsend[...] = (acc[pl.ds(UNITS, UNITS)] + part).astype(jnp.bfloat16)
    for c in range(N_CHUNK):
        g_copy(c).start()
    acc[pl.ds(0, UNITS)] += partial(1, 1, 0, UNITS)
    for load in loads[5:]:
        load.wait()

    mine = pl.ds(pl.multiple_of(rep * COLS, COLS), COLS)

    def rs_copy(c, k):
        rows = pl.ds(c * CHUNK, CHUNK)
        cols = pl.ds(pl.multiple_of(((rep + k) % REP) * COLS, COLS), COLS)
        return remote(diff_b.at[rows, cols], rs.at[k - 1, rows], ss, sr.at[c], peers[k - 1])

    def ag_copy(c, k):
        rows = pl.ds(c * CHUNK, CHUNK)
        return remote(ag.at[rows, mine], ag.at[rows, mine], as_, ar.at[c], peers[k - 1])

    def sum_chunk(c):
        rows = pl.ds(c * CHUNK, CHUNK)
        wait_bytes(rs.at[:, rows], sr.at[c])
        total = diff[rows, mine]
        for k in range(1, REP):
            total += rs[k - 1, rows].astype(jnp.float32)
        ag[rows, mine] = (total / REP).astype(jnp.bfloat16)
        for k in range(1, REP):
            ag_copy(c, k).start()

    for c in range(N_CHUNK):
        rows = pl.ds(c * CHUNK, CHUNK)
        g_copy(c).wait_recv()
        grad = (acc[rows] + grecv[rows].astype(jnp.float32)) * in_scale
        grad_v[rows] = grad
        moment_new = beta_first * first_v[rows] + (1.0 - beta_first) * grad
        second_new = beta_second * second_v[rows] + (1.0 - beta_second) * grad * grad
        direction = moment_new / bias_first / (jnp.sqrt(second_new / bias_second) + adam_floor)
        gate_value = wp[rows].astype(jnp.float32)
        inner = gate_value * (1.0 - inner_rate * decay_rate) - inner_rate * direction
        difference = base_v[rows].astype(jnp.float32) - inner
        diff[rows] = difference
        diff_b[rows] = difference.astype(jnp.bfloat16)
        for k in range(1, REP):
            rs_copy(c, k).start()
        pltpu.make_async_copy(grad_v.at[rows], grad_out.at[rows], out_sem.at[0]).start()
        if c > 0:
            sum_chunk(c - 1)
    sum_chunk(N_CHUNK - 1)

    for c in range(N_CHUNK):
        rows = pl.ds(c * CHUNK, CHUNK)
        wait_bytes(ag.at[rows, pl.ds(0, D - COLS)], ar.at[c])
        pltpu.make_async_copy(ag.at[rows], total_out.at[rows], out_sem.at[1]).start()

    z_sends = sum(goes(w, yy, h, p) for w in range(2) for yy in range(2) for h in range(1, 5) for p in range(PIECES))
    wait_bytes(xg.at[0, pl.ds(0, z_sends * PIECE)], zs)
    wait_bytes(xg.at[0], cs)
    wait_bytes(xg.at[0, pl.ds(0, Y_FIRST * PIECE)], ys)
    wait_bytes(xg.at[0, pl.ds(0, NZ * PIECE)], ls)
    wait_bytes(wp.at[pl.ds(0, 3 * UNITS)], ws)
    wait_bytes(gsend, gs)
    wait_bytes(diff_b.at[:, pl.ds(0, D - COLS)], ss)
    wait_bytes(diff_b.at[:, pl.ds(0, D - COLS)], as_)
    wait_bytes(grad_v, out_sem.at[0])
    wait_bytes(ag, out_sem.at[1])


def on_device(
    tokens_in,
    out_grad,
    gate_weight,
    up_weight,
    down_weight,
    base_gate,
    first_moment,
    second_moment,
    outer_momentum,
):
    dma = pltpu.SemaphoreType.DMA
    f32, bf16 = jnp.float32, jnp.bfloat16
    grad, total = pl.pallas_call(
        kernel,
        out_shape=[jax.ShapeDtypeStruct((UNITS, D), f32), jax.ShapeDtypeStruct((UNITS, D), bf16)],
        in_specs=[pl.BlockSpec(memory_space=pl.ANY)] * 8,
        out_specs=[pl.BlockSpec(memory_space=pl.ANY)] * 2,
        scratch_shapes=[
            pltpu.VMEM((2, NZ * SLOT, D), bf16),
            pltpu.VMEM((4 * UNITS, D), bf16),
            pltpu.VMEM((2 * UNITS, D), bf16),
            pltpu.VMEM((2 * UNITS, NZ * SLOT), f32),
            pltpu.VMEM((2 * UNITS, D), f32),
            pltpu.VMEM((UNITS, D), bf16),
            pltpu.VMEM((UNITS, D), f32),
            pltpu.VMEM((UNITS, D), f32),
            pltpu.VMEM((UNITS, D), bf16),
            pltpu.VMEM((UNITS, D), bf16),
            pltpu.VMEM((UNITS, D), f32),
            pltpu.VMEM((UNITS, D), f32),
            pltpu.VMEM((UNITS, D), bf16),
            pltpu.VMEM((REP - 1, UNITS, COLS), bf16),
            pltpu.VMEM((UNITS, D), bf16),
            dma((4,)),
            dma,
            dma((2, 2, NZ // 2, PIECES)),
            dma,
            dma((NZ,)),
            dma,
            dma((Y_FIRST,)),
            dma,
            dma((NZ,)),
            dma,
            dma((2,)),
            dma,
            dma((N_CHUNK,)),
            dma,
            dma((N_CHUNK,)),
            dma,
            dma((N_CHUNK,)),
            dma((2,)),
        ],
        compiler_params=pltpu.CompilerParams(
            collective_id=0, has_side_effects=True, vmem_limit_bytes=60 * 2**20
        ),
        name="window",
    )(
        tokens_in,
        out_grad,
        gate_weight,
        up_weight,
        down_weight,
        base_gate,
        first_moment,
        second_moment,
    )
    outer_grad = total.astype(f32)
    moment_new = beta_first * first_moment[0] + (1.0 - beta_first) * grad
    second_new = beta_second * second_moment[0] + (1.0 - beta_second) * grad * grad
    new_momentum = nesterov_factor * outer_momentum + outer_grad
    base_value = base_gate.astype(jnp.float32)
    new_base = base_value - outer_rate * (outer_grad + nesterov_factor * new_momentum)
    return (new_base, new_momentum, moment_new[None], second_new[None])


def solution(mesh):
    in_specs = (
        P("rep", "fsdp", None),
        P("rep", "fsdp", None),
        P("rep", "fsdp", None),
        P("rep", "fsdp", None),
        P("rep", "fsdp", None),
        P("fsdp", None),
        P("rep", "fsdp", None),
        P("rep", "fsdp", None),
        P("fsdp", None),
    )
    out_specs = (P("fsdp", None), P("fsdp", None), P("rep", "fsdp", None), P("rep", "fsdp", None))
    return jax.shard_map(
        on_device, mesh=mesh, in_specs=in_specs, out_specs=out_specs, check_vma=False
    )
```

```python
import math

import jax
import jax.numpy as jnp
from jax import lax
from jax.experimental import pallas as pl
from jax.experimental.pallas import tpu as pltpu
from jax.sharding import PartitionSpec as P

inner_rate = 0.02
beta_first = 0.9
beta_second = 0.95
adam_floor = 1e-08
decay_rate = 0.1
bias_first = 1.0 - 0.9**20
bias_second = 1.0 - 0.95**20
nesterov_factor = 0.9
outer_rate = 0.7

MESH = pl.DeviceIdType.MESH
NZ, NY, REP = 8, 4, 8
ROWS, UNITS, D = 32, 64, 2048
SLOT = 4 * ROWS
PIECE = 16
PIECES = 4
Y_FIRST = 3
CHUNK = 32
N_CHUNK = UNITS // CHUNK
COLS = D // REP

in_scale = 1.0 / math.sqrt(D)
out_scale = 1.0 / math.sqrt(UNITS * NZ * NY * 2)


def place(way, hops):
    if hops == 0:
        return 0
    if hops == NZ // 2:
        return 1
    return 2 * hops + way


def kernel(
    tokens, grads, gate, up, down, base, first, second,
    grad_out, total_out,
    xg, wp, wd, held_v, acc, base_v, first_v, second_v, gsend, grecv, diff, diff_b, rs, ag,
    load_sem, zs, zr, cs, cr, ys, yr, ls, lr, ws, wr, gs, gr, ss, sr, as_, ar,
):
    rep = lax.axis_index("rep")
    me = lax.axis_index("fsdp")
    z = me // (2 * NY)
    y = (me // 2) % NY
    core = me % 2

    def at(z_, y_, core_):
        return (rep, (z_ * NY + y_) * 2 + core_)

    z_next = (at((z + 1) % NZ, y, core), at((z + NZ - 1) % NZ, y, core))
    sibling = at(z, y, 1 - core)
    token_pair = at(z, y + 1 - 2 * (y % 2), core)
    weight_pair = at(z, (y + 3 + 2 * (y % 2)) % NY, core)
    peers = [((rep + k) % REP, me) for k in range(1, REP)]

    loads = [
        pltpu.make_async_copy(src, dst, load_sem.at[i])
        for src, dst, i in [
            (tokens.at[0], xg.at[0, pl.ds(0, ROWS)], 0),
            (grads.at[0], xg.at[1, pl.ds(0, ROWS)], 0),
            (gate.at[0], wp.at[pl.ds(0, UNITS)], 0),
            (up.at[0], wp.at[pl.ds(2 * UNITS, UNITS)], 0),
            (down.at[0], wd.at[pl.ds(0, UNITS)], 0),
            (base, base_v, 1),
            (first.at[0], first_v, 2),
            (second.at[0], second_v, 3),
        ]
    ]
    for load in loads:
        load.start()

    barrier = pltpu.get_barrier_semaphore()
    others = [*z_next, sibling, token_pair, weight_pair, *peers]
    for other in others:
        pl.semaphore_signal(barrier, inc=1, device_id=other, device_id_type=MESH)
    pltpu.make_async_copy(wp, wp, load_sem.at[0]).wait()
    pl.semaphore_wait(barrier, len(others))

    def remote(src, dst, send, recv, device):
        return pltpu.make_async_remote_copy(
            src_ref=src, dst_ref=dst, send_sem=send, recv_sem=recv, device_id=device, device_id_type=MESH
        )

    def wait_bytes(ref, sem):
        pltpu.make_async_copy(ref, ref, sem).wait()

    def shard(slot, yy, cc, p):
        row = slot * SLOT + yy * 2 * ROWS + cc * ROWS + p % 2 * PIECE
        return xg.at[p // 2, pl.ds(row, PIECE)]

    def goes(way, yy, hops, p):
        if yy == 1 and p >= Y_FIRST:
            return False
        return hops < NZ // 2 or (hops == NZ // 2 and (p >= (PIECES - yy) // 2) == way)

    def z_copy(way, yy, hops, p):
        return remote(
            shard(place(way, hops - 1), yy, 0, p),
            shard(place(way, hops), yy, 0, p),
            zs,
            zr.at[way, yy, hops - 1, p],
            z_next[way],
        )

    def core_copy(slot, yy, p):
        return remote(shard(slot, yy, 0, p), shard(slot, yy, 1, p), cs, cr.at[slot], sibling)

    def y_copy(p):
        return remote(shard(0, 0, 0, p), shard(0, 1, 0, p), ys, yr.at[p], token_pair)

    def late_copy(slot):
        return remote(shard(slot, 0, 0, Y_FIRST), shard(slot, 1, 0, Y_FIRST), ls, lr.at[slot], token_pair)

    def w_copy(i):
        ref, row = ((wp, 0), (wp, 2 * UNITS), (wd, 0))[i]
        return remote(ref.at[pl.ds(row, UNITS)], ref.at[pl.ds(row + UNITS, UNITS)], ws, wr.at[i // 2], weight_pair)

    order = (*range(Y_FIRST, PIECES), *range(Y_FIRST))
    for p in order:
        if p < Y_FIRST:
            y_copy(p).start()
        for way in range(2):
            z_copy(way, 0, 1, p).start()
    late_copy(0).start()
    for i in range(3):
        w_copy(i).start()
    for p in range(PIECES):
        core_copy(0, 0, p).start()

    def arrive(yy, hops):
        for p in order:
            for way in range(2):
                if not goes(way, yy, hops, p):
                    continue
                slot = place(way, hops)
                z_copy(way, yy, hops, p).wait_recv()
                if goes(way, yy, hops + 1, p):
                    z_copy(way, yy, hops + 1, p).start()
                if p >= Y_FIRST:
                    late_copy(slot).start()
                core_copy(slot, yy, p).start()

    def arrive_y():
        for p in range(Y_FIRST):
            y_copy(p).wait_recv()
            for way in range(2):
                z_copy(way, 1, 1, p).start()
            core_copy(0, 1, p).start()

    def arrive_late(hops):
        for way in range(2):
            if goes(way, 0, hops, Y_FIRST) and (hops > 0 or way == 0):
                slot = place(way, hops)
                late_copy(slot).wait_recv()
                core_copy(slot, 1, Y_FIRST).start()

    nt = (((1,), (1,)), ((), ()))

    def settle(slot, slots):
        for s in range(slot, slot + slots):
            wait_bytes(xg.at[0, pl.ds(0, SLOT)], cr.at[s])

    def gain(slot, slots, unit, units):
        x = xg[0, pl.ds(slot * SLOT, slots * SLOT)]
        if units == 2 * UNITS:
            both = lax.dot_general(wp[...], x, nt, preferred_element_type=jnp.float32) * in_scale
            pre, lin = both[:units], both[units:]
        else:
            pre = lax.dot_general(wp[pl.ds(unit, units)], x, nt, preferred_element_type=jnp.float32) * in_scale
            lin = lax.dot_general(wp[pl.ds(2 * UNITS + unit, units)], x, nt, preferred_element_type=jnp.float32) * in_scale
        sig = jax.nn.sigmoid(pre)
        return lin, sig, 1.0 + pre * (1.0 - sig)

    def slope(slot, slots, unit, units, held):
        rows = pl.ds(slot * SLOT, slots * SLOT)
        back = lax.dot_general(wd[pl.ds(unit, units)], xg[1, rows], nt, preferred_element_type=jnp.float32) * out_scale
        lin, sig, rest = held
        dpre = (back * lin * sig * rest).astype(jnp.bfloat16)
        return jnp.dot(dpre, xg[0, rows], preferred_element_type=jnp.float32)

    def partial(slot, slots, unit, units):
        return slope(slot, slots, unit, units, gain(slot, slots, unit, units))

    def early(slot, slots):
        settle(slot, slots)
        lin, sig, rest = gain(slot, slots, 0, 2 * UNITS)
        cols = pl.ds(slot * SLOT, slots * SLOT)
        held_v[:, cols] = lin * sig * rest

    def late(slot, slots, begin=False):
        rows = pl.ds(slot * SLOT, slots * SLOT)
        back = lax.dot_general(wd[...], xg[1, rows], nt, preferred_element_type=jnp.float32) * out_scale
        dpre = (back * held_v[:, rows]).astype(jnp.bfloat16)
        part = jnp.dot(dpre, xg[0, rows], preferred_element_type=jnp.float32)
        if begin:
            acc[...] = part
        else:
            acc[...] += part

    def block(slot, slots, begin=False):
        settle(slot, slots)
        part = partial(slot, slots, 0, 2 * UNITS)
        if begin:
            acc[...] = part
        else:
            acc[...] += part

    arrive(0, 1)
    arrive(0, 2)
    arrive_y()
    arrive_late(0)
    arrive(0, 3)
    arrive_late(1)
    arrive(1, 1)
    arrive(0, 4)
    arrive_late(2)
    wait_bytes(wd, wr.at[0])
    early(0, 1)
    arrive(1, 2)
    early(2, 2)
    early(4, 2)
    w_copy(2).wait_recv()
    late(0, 1, True)
    arrive_late(3)
    arrive(1, 3)
    late(2, 2)
    late(4, 2)
    block(6, 2)
    arrive_late(4)
    arrive(1, 4)

    def g_copy(c):
        rows = pl.ds(c * CHUNK, CHUNK)
        return remote(gsend.at[rows], grecv.at[rows], gs, gr.at[c], weight_pair)

    settle(1, 1)
    part = partial(1, 1, UNITS, UNITS)
    gsend[...] = (acc[pl.ds(UNITS, UNITS)] + part).astype(jnp.bfloat16)
    for c in range(N_CHUNK):
        g_copy(c).start()
    acc[pl.ds(0, UNITS)] += partial(1, 1, 0, UNITS)
    for load in loads[5:]:
        load.wait()

    mine = pl.ds(pl.multiple_of(rep * COLS, COLS), COLS)

    def rs_copy(c, k):
        rows = pl.ds(c * CHUNK, CHUNK)
        cols = pl.ds(pl.multiple_of(((rep + k) % REP) * COLS, COLS), COLS)
        return remote(diff_b.at[rows, cols], rs.at[k - 1, rows], ss, sr.at[c], peers[k - 1])

    def ag_copy(c, k):
        rows = pl.ds(c * CHUNK, CHUNK)
        return remote(ag.at[rows, mine], ag.at[rows, mine], as_, ar.at[c], peers[k - 1])

    def sum_chunk(c):
        rows = pl.ds(c * CHUNK, CHUNK)
        wait_bytes(rs.at[:, rows], sr.at[c])
        total = diff[rows, mine]
        for k in range(1, REP):
            total += rs[k - 1, rows].astype(jnp.float32)
        ag[rows, mine] = (total / REP).astype(jnp.bfloat16)
        for k in range(1, REP):
            ag_copy(c, k).start()

    for c in range(N_CHUNK):
        rows = pl.ds(c * CHUNK, CHUNK)
        g_copy(c).wait_recv()
        grad = (acc[rows] + grecv[rows].astype(jnp.float32)) * in_scale
        grad_out[rows] = grad
        moment_new = beta_first * first_v[rows] + (1.0 - beta_first) * grad
        second_new = beta_second * second_v[rows] + (1.0 - beta_second) * grad * grad
        direction = moment_new / bias_first / (jnp.sqrt(second_new / bias_second) + adam_floor)
        gate_value = wp[rows].astype(jnp.float32)
        inner = gate_value * (1.0 - inner_rate * decay_rate) - inner_rate * direction
        difference = base_v[rows].astype(jnp.float32) - inner
        diff[rows] = difference
        diff_b[rows] = difference.astype(jnp.bfloat16)
        for k in range(1, REP):
            rs_copy(c, k).start()
        if c > 0:
            sum_chunk(c - 1)
    sum_chunk(N_CHUNK - 1)

    for c in range(N_CHUNK):
        rows = pl.ds(c * CHUNK, CHUNK)
        wait_bytes(ag.at[rows, pl.ds(0, D - COLS)], ar.at[c])
        total_out[rows] = ag[rows]

    z_sends = sum(goes(w, yy, h, p) for w in range(2) for yy in range(2) for h in range(1, 5) for p in range(PIECES))
    wait_bytes(xg.at[0, pl.ds(0, z_sends * PIECE)], zs)
    wait_bytes(xg.at[0], cs)
    wait_bytes(xg.at[0, pl.ds(0, Y_FIRST * PIECE)], ys)
    wait_bytes(xg.at[0, pl.ds(0, NZ * PIECE)], ls)
    wait_bytes(wp.at[pl.ds(0, 3 * UNITS)], ws)
    wait_bytes(gsend, gs)
    wait_bytes(diff_b.at[:, pl.ds(0, D - COLS)], ss)
    wait_bytes(diff_b.at[:, pl.ds(0, D - COLS)], as_)


def on_device(
    tokens_in,
    out_grad,
    gate_weight,
    up_weight,
    down_weight,
    base_gate,
    first_moment,
    second_moment,
    outer_momentum,
):
    dma = pltpu.SemaphoreType.DMA
    f32, bf16 = jnp.float32, jnp.bfloat16
    grad, total = pl.pallas_call(
        kernel,
        out_shape=[pltpu.VMEM((UNITS, D), f32), pltpu.VMEM((UNITS, D), bf16)],
        in_specs=[pl.BlockSpec(memory_space=pl.ANY)] * 8,
        out_specs=[pl.BlockSpec(memory_space=pltpu.VMEM)] * 2,
        scratch_shapes=[
            pltpu.VMEM((2, NZ * SLOT, D), bf16),
            pltpu.VMEM((4 * UNITS, D), bf16),
            pltpu.VMEM((2 * UNITS, D), bf16),
            pltpu.VMEM((2 * UNITS, NZ * SLOT), f32),
            pltpu.VMEM((2 * UNITS, D), f32),
            pltpu.VMEM((UNITS, D), bf16),
            pltpu.VMEM((UNITS, D), f32),
            pltpu.VMEM((UNITS, D), f32),
            pltpu.VMEM((UNITS, D), bf16),
            pltpu.VMEM((UNITS, D), bf16),
            pltpu.VMEM((UNITS, D), f32),
            pltpu.VMEM((UNITS, D), bf16),
            pltpu.VMEM((REP - 1, UNITS, COLS), bf16),
            pltpu.VMEM((UNITS, D), bf16),
            dma((4,)),
            dma,
            dma((2, 2, NZ // 2, PIECES)),
            dma,
            dma((NZ,)),
            dma,
            dma((Y_FIRST,)),
            dma,
            dma((NZ,)),
            dma,
            dma((2,)),
            dma,
            dma((N_CHUNK,)),
            dma,
            dma((N_CHUNK,)),
            dma,
            dma((N_CHUNK,)),
        ],
        compiler_params=pltpu.CompilerParams(
            collective_id=0, has_side_effects=True, vmem_limit_bytes=54 * 2**20
        ),
        name="window",
    )(
        tokens_in,
        out_grad,
        gate_weight,
        up_weight,
        down_weight,
        base_gate,
        first_moment,
        second_moment,
    )
    outer_grad = total.astype(f32)
    moment_new = beta_first * first_moment[0] + (1.0 - beta_first) * grad
    second_new = beta_second * second_moment[0] + (1.0 - beta_second) * grad * grad
    new_momentum = nesterov_factor * outer_momentum + outer_grad
    base_value = base_gate.astype(jnp.float32)
    new_base = base_value - outer_rate * (outer_grad + nesterov_factor * new_momentum)
    return (new_base, new_momentum, moment_new[None], second_new[None])


def solution(mesh):
    in_specs = (
        P("rep", "fsdp", None),
        P("rep", "fsdp", None),
        P("rep", "fsdp", None),
        P("rep", "fsdp", None),
        P("rep", "fsdp", None),
        P("fsdp", None),
        P("rep", "fsdp", None),
        P("rep", "fsdp", None),
        P("fsdp", None),
    )
    out_specs = (P("fsdp", None), P("fsdp", None), P("rep", "fsdp", None), P("rep", "fsdp", None))
    return jax.shard_map(
        on_device, mesh=mesh, in_specs=in_specs, out_specs=out_specs, check_vma=False
    )
```

```python
import math

import jax
import jax.numpy as jnp
from jax import lax
from jax.experimental import pallas as pl
from jax.experimental.pallas import tpu as pltpu
from jax.sharding import PartitionSpec as P

inner_rate = 0.02
beta_first = 0.9
beta_second = 0.95
adam_floor = 1e-08
decay_rate = 0.1
bias_first = 1.0 - 0.9**20
bias_second = 1.0 - 0.95**20
nesterov_factor = 0.9
outer_rate = 0.7

MESH = pl.DeviceIdType.MESH
NZ, NY, REP = 8, 4, 8
ROWS, UNITS, D = 32, 64, 2048
SLOT = 4 * ROWS
PIECE = 16
PIECES = 4
Y_FIRST = 3
CHUNK = 32
N_CHUNK = UNITS // CHUNK
COLS = D // REP

in_scale = 1.0 / math.sqrt(D)
out_scale = 1.0 / math.sqrt(UNITS * NZ * NY * 2)


def place(way, hops):
    if hops == 0:
        return 0
    if hops == NZ // 2:
        return 1
    return 2 * hops + way


def kernel(
    tokens, grads, gate, up, down, base, first, second,
    grad_out, total_out,
    xg, wp, wd, held_v, acc, base_v, first_v, second_v, gsend, grecv, diff, diff_b, rs, ag,
    load_sem, zs, zr, cs, cr, ys, yr, ls, lr, ws, wr, gs, gr, ss, sr, as_, ar,
):
    rep = lax.axis_index("rep")
    me = lax.axis_index("fsdp")
    z = me // (2 * NY)
    y = (me // 2) % NY
    core = me % 2

    def at(z_, y_, core_):
        return (rep, (z_ * NY + y_) * 2 + core_)

    z_next = (at((z + 1) % NZ, y, core), at((z + NZ - 1) % NZ, y, core))
    sibling = at(z, y, 1 - core)
    token_pair = at(z, y + 1 - 2 * (y % 2), core)
    weight_pair = at(z, (y + 3 + 2 * (y % 2)) % NY, core)
    peers = [((rep + k) % REP, me) for k in range(1, REP)]
    far_first = (4, 3, 5, 2, 6, 1, 7)

    loads = [
        pltpu.make_async_copy(src, dst, load_sem.at[i])
        for src, dst, i in [
            (tokens.at[0], xg.at[0, pl.ds(0, ROWS)], 0),
            (grads.at[0], xg.at[1, pl.ds(0, ROWS)], 0),
            (gate.at[0], wp.at[pl.ds(0, UNITS)], 0),
            (up.at[0], wp.at[pl.ds(2 * UNITS, UNITS)], 0),
            (down.at[0], wd.at[pl.ds(0, UNITS)], 0),
            (base, base_v, 1),
            (first.at[0], first_v, 2),
            (second.at[0], second_v, 3),
        ]
    ]
    for load in loads:
        load.start()

    barrier = pltpu.get_barrier_semaphore()
    others = [*z_next, sibling, token_pair, weight_pair, *peers]
    for other in others:
        pl.semaphore_signal(barrier, inc=1, device_id=other, device_id_type=MESH)
    pltpu.make_async_copy(wp, wp, load_sem.at[0]).wait()
    pl.semaphore_wait(barrier, len(others))

    def remote(src, dst, send, recv, device):
        return pltpu.make_async_remote_copy(
            src_ref=src, dst_ref=dst, send_sem=send, recv_sem=recv, device_id=device, device_id_type=MESH
        )

    def wait_bytes(ref, sem):
        pltpu.make_async_copy(ref, ref, sem).wait()

    def shard(slot, yy, cc, p):
        row = slot * SLOT + yy * 2 * ROWS + cc * ROWS + p % 2 * PIECE
        return xg.at[p // 2, pl.ds(row, PIECE)]

    def goes(way, yy, hops, p):
        if yy == 1 and p >= Y_FIRST:
            return False
        return hops < NZ // 2 or (hops == NZ // 2 and (p >= (PIECES - yy) // 2) == way)

    def z_copy(way, yy, hops, p):
        return remote(
            shard(place(way, hops - 1), yy, 0, p),
            shard(place(way, hops), yy, 0, p),
            zs,
            zr.at[way, yy, hops - 1, p],
            z_next[way],
        )

    def core_copy(slot, yy, p):
        return remote(shard(slot, yy, 0, p), shard(slot, yy, 1, p), cs, cr.at[slot, p // 2], sibling)

    def y_copy(p):
        return remote(shard(0, 0, 0, p), shard(0, 1, 0, p), ys, yr.at[p], token_pair)

    def late_copy(slot):
        return remote(shard(slot, 0, 0, Y_FIRST), shard(slot, 1, 0, Y_FIRST), ls, lr.at[slot], token_pair)

    def w_copy(i):
        ref, row = ((wp, 0), (wp, 2 * UNITS), (wd, 0))[i]
        return remote(ref.at[pl.ds(row, UNITS)], ref.at[pl.ds(row + UNITS, UNITS)], ws, wr.at[i // 2], weight_pair)

    order = (*range(Y_FIRST, PIECES), *range(Y_FIRST))
    for p in order:
        if p < Y_FIRST:
            y_copy(p).start()
        for way in range(2):
            z_copy(way, 0, 1, p).start()
    late_copy(0).start()
    for i in range(3):
        w_copy(i).start()
    for p in range(PIECES):
        core_copy(0, 0, p).start()

    def arrive(yy, hops):
        for p in order:
            for way in range(2):
                if not goes(way, yy, hops, p):
                    continue
                slot = place(way, hops)
                z_copy(way, yy, hops, p).wait_recv()
                if goes(way, yy, hops + 1, p):
                    z_copy(way, yy, hops + 1, p).start()
                if p >= Y_FIRST:
                    late_copy(slot).start()
                core_copy(slot, yy, p).start()

    def arrive_y():
        for p in range(Y_FIRST):
            y_copy(p).wait_recv()
            for way in range(2):
                z_copy(way, 1, 1, p).start()
            core_copy(0, 1, p).start()

    def arrive_late(hops):
        for way in range(2):
            if goes(way, 0, hops, Y_FIRST) and (hops > 0 or way == 0):
                slot = place(way, hops)
                late_copy(slot).wait_recv()
                core_copy(slot, 1, Y_FIRST).start()

    nt = (((1,), (1,)), ((), ()))

    def settle(slot, slots):
        for s in range(slot, slot + slots):
            for kind in range(2):
                wait_bytes(xg.at[0, pl.ds(0, SLOT // 2)], cr.at[s, kind])

    def gain(slot, slots, unit, units):
        x = xg[0, pl.ds(slot * SLOT, slots * SLOT)]
        if units == 2 * UNITS:
            both = lax.dot_general(wp[...], x, nt, preferred_element_type=jnp.float32) * in_scale
            pre, lin = both[:units], both[units:]
        else:
            pre = lax.dot_general(wp[pl.ds(unit, units)], x, nt, preferred_element_type=jnp.float32) * in_scale
            lin = lax.dot_general(wp[pl.ds(2 * UNITS + unit, units)], x, nt, preferred_element_type=jnp.float32) * in_scale
        sig = jax.nn.sigmoid(pre)
        return lin, sig, 1.0 + pre * (1.0 - sig)

    def slope(slot, slots, unit, units, held):
        rows = pl.ds(slot * SLOT, slots * SLOT)
        back = lax.dot_general(wd[pl.ds(unit, units)], xg[1, rows], nt, preferred_element_type=jnp.float32) * out_scale
        lin, sig, rest = held
        dpre = (back * lin * sig * rest).astype(jnp.bfloat16)
        return jnp.dot(dpre, xg[0, rows], preferred_element_type=jnp.float32)

    def partial(slot, slots, unit, units):
        return slope(slot, slots, unit, units, gain(slot, slots, unit, units))

    def early(slot, slots):
        settle(slot, slots)
        lin, sig, rest = gain(slot, slots, 0, 2 * UNITS)
        cols = pl.ds(slot * SLOT, slots * SLOT)
        held_v[:, cols] = lin * sig * rest

    def late(slot, slots, begin=False):
        rows = pl.ds(slot * SLOT, slots * SLOT)
        back = lax.dot_general(wd[...], xg[1, rows], nt, preferred_element_type=jnp.float32) * out_scale
        dpre = (back * held_v[:, rows]).astype(jnp.bfloat16)
        part = jnp.dot(dpre, xg[0, rows], preferred_element_type=jnp.float32)
        if begin:
            acc[...] = part
        else:
            acc[...] += part

    def block(slot, slots, begin=False):
        settle(slot, slots)
        part = partial(slot, slots, 0, 2 * UNITS)
        if begin:
            acc[...] = part
        else:
            acc[...] += part

    arrive(0, 1)
    arrive(0, 2)
    arrive_y()
    arrive(0, 3)
    arrive(1, 1)
    arrive_late(0)
    arrive_late(1)
    arrive(0, 4)
    wait_bytes(wd, wr.at[0])
    early(0, 1)
    arrive(1, 2)
    arrive_late(2)
    early(2, 2)
    early(4, 2)
    w_copy(2).wait_recv()
    late(0, 1, True)
    arrive(1, 3)
    arrive_late(3)
    late(2, 2)
    late(4, 2)
    block(6, 2)
    arrive_late(4)
    arrive(1, 4)

    def g_copy(c):
        rows = pl.ds(c * CHUNK, CHUNK)
        return remote(gsend.at[rows], grecv.at[rows], gs, gr.at[c], weight_pair)

    wait_bytes(xg.at[0, pl.ds(0, SLOT // 2)], cr.at[1, 0])
    held = gain(1, 1, UNITS, UNITS)
    wait_bytes(xg.at[0, pl.ds(0, SLOT // 2)], cr.at[1, 1])
    part = slope(1, 1, UNITS, UNITS, held)
    gsend[...] = (acc[pl.ds(UNITS, UNITS)] + part).astype(jnp.bfloat16)
    for c in range(N_CHUNK):
        g_copy(c).start()
    acc[pl.ds(0, UNITS)] += partial(1, 1, 0, UNITS)
    for load in loads[5:]:
        load.wait()
    own = pl.ds(0, UNITS)
    acc[own] = acc[own] * in_scale
    diff[...] = base_v[...].astype(jnp.float32) - wp[own].astype(jnp.float32) * (1.0 - inner_rate * decay_rate)

    mine = pl.ds(pl.multiple_of(rep * COLS, COLS), COLS)

    def rs_copy(c, k):
        rows = pl.ds(c * CHUNK, CHUNK)
        cols = pl.ds(pl.multiple_of(((rep + k) % REP) * COLS, COLS), COLS)
        return remote(diff_b.at[rows, cols], rs.at[k - 1, rows], ss, sr.at[c], peers[k - 1])

    def ag_copy(c, k):
        rows = pl.ds(c * CHUNK, CHUNK)
        return remote(ag.at[rows, mine], ag.at[rows, mine], as_, ar.at[c], peers[k - 1])

    def sum_chunk(c):
        rows = pl.ds(c * CHUNK, CHUNK)
        wait_bytes(rs.at[:, rows], sr.at[c])
        total = diff[rows, mine]
        for k in range(1, REP):
            total += rs[k - 1, rows].astype(jnp.float32)
        ag[rows, mine] = (total / REP).astype(jnp.bfloat16)
        for k in far_first:
            ag_copy(c, k).start()

    for c in range(N_CHUNK):
        rows = pl.ds(c * CHUNK, CHUNK)
        g_copy(c).wait_recv()
        grad = acc[rows] + grecv[rows].astype(jnp.float32) * in_scale
        grad_out[rows] = grad
        moment_new = beta_first * first_v[rows] + (1.0 - beta_first) * grad
        second_new = beta_second * second_v[rows] + (1.0 - beta_second) * grad * grad
        direction = moment_new * (1.0 / bias_first) / (jnp.sqrt(second_new * (1.0 / bias_second)) + adam_floor)
        difference = diff[rows] + inner_rate * direction
        diff[rows] = difference
        diff_b[rows] = difference.astype(jnp.bfloat16)
        for k in far_first:
            rs_copy(c, k).start()
        if c > 0:
            sum_chunk(c - 1)
    sum_chunk(N_CHUNK - 1)

    for c in range(N_CHUNK):
        rows = pl.ds(c * CHUNK, CHUNK)
        wait_bytes(ag.at[rows, pl.ds(0, D - COLS)], ar.at[c])
        total_out[rows] = ag[rows]

    z_sends = sum(goes(w, yy, h, p) for w in range(2) for yy in range(2) for h in range(1, 5) for p in range(PIECES))
    wait_bytes(xg.at[0, pl.ds(0, z_sends * PIECE)], zs)
    wait_bytes(xg.at[0], cs)
    wait_bytes(xg.at[0, pl.ds(0, Y_FIRST * PIECE)], ys)
    wait_bytes(xg.at[0, pl.ds(0, NZ * PIECE)], ls)
    wait_bytes(wp.at[pl.ds(0, 3 * UNITS)], ws)
    wait_bytes(gsend, gs)
    wait_bytes(diff_b.at[:, pl.ds(0, D - COLS)], ss)
    wait_bytes(diff_b.at[:, pl.ds(0, D - COLS)], as_)


def on_device(
    tokens_in,
    out_grad,
    gate_weight,
    up_weight,
    down_weight,
    base_gate,
    first_moment,
    second_moment,
    outer_momentum,
):
    dma = pltpu.SemaphoreType.DMA
    f32, bf16 = jnp.float32, jnp.bfloat16
    grad, total = pl.pallas_call(
        kernel,
        out_shape=[pltpu.VMEM((UNITS, D), f32), pltpu.VMEM((UNITS, D), bf16)],
        in_specs=[pl.BlockSpec(memory_space=pl.ANY)] * 8,
        out_specs=[pl.BlockSpec(memory_space=pltpu.VMEM)] * 2,
        scratch_shapes=[
            pltpu.VMEM((2, NZ * SLOT, D), bf16),
            pltpu.VMEM((4 * UNITS, D), bf16),
            pltpu.VMEM((2 * UNITS, D), bf16),
            pltpu.VMEM((2 * UNITS, NZ * SLOT), f32),
            pltpu.VMEM((2 * UNITS, D), f32),
            pltpu.VMEM((UNITS, D), bf16),
            pltpu.VMEM((UNITS, D), f32),
            pltpu.VMEM((UNITS, D), f32),
            pltpu.VMEM((UNITS, D), bf16),
            pltpu.VMEM((UNITS, D), bf16),
            pltpu.VMEM((UNITS, D), f32),
            pltpu.VMEM((UNITS, D), bf16),
            pltpu.VMEM((REP - 1, UNITS, COLS), bf16),
            pltpu.VMEM((UNITS, D), bf16),
            dma((4,)),
            dma,
            dma((2, 2, NZ // 2, PIECES)),
            dma,
            dma((NZ, 2)),
            dma,
            dma((Y_FIRST,)),
            dma,
            dma((NZ,)),
            dma,
            dma((2,)),
            dma,
            dma((N_CHUNK,)),
            dma,
            dma((N_CHUNK,)),
            dma,
            dma((N_CHUNK,)),
        ],
        compiler_params=pltpu.CompilerParams(
            collective_id=0, has_side_effects=True, vmem_limit_bytes=54 * 2**20
        ),
        name="window",
    )(
        tokens_in,
        out_grad,
        gate_weight,
        up_weight,
        down_weight,
        base_gate,
        first_moment,
        second_moment,
    )
    outer_grad = total.astype(f32)
    moment_new = beta_first * first_moment[0] + (1.0 - beta_first) * grad
    second_new = beta_second * second_moment[0] + (1.0 - beta_second) * grad * grad
    new_momentum = nesterov_factor * outer_momentum + outer_grad
    base_value = base_gate.astype(jnp.float32)
    new_base = base_value - outer_rate * (outer_grad + nesterov_factor * new_momentum)
    return (new_base, new_momentum, moment_new[None], second_new[None])


def solution(mesh):
    in_specs = (
        P("rep", "fsdp", None),
        P("rep", "fsdp", None),
        P("rep", "fsdp", None),
        P("rep", "fsdp", None),
        P("rep", "fsdp", None),
        P("fsdp", None),
        P("rep", "fsdp", None),
        P("rep", "fsdp", None),
        P("fsdp", None),
    )
    out_specs = (P("fsdp", None), P("fsdp", None), P("rep", "fsdp", None), P("rep", "fsdp", None))
    return jax.shard_map(
        on_device, mesh=mesh, in_specs=in_specs, out_specs=out_specs, check_vma=False
    )
```
